256 devices in a mesh: section: 8 (over z_hi, core), expert: 32 (over z_lo, x, y).
Axes of the slice: x: 4, y: 4, z: 8 (z_hi: 4, z_lo: 2; z = z_hi * 2 + z_lo), core: 2. Of those that a mesh axis runs over, the one named last changes fastest.
Arguments:
- tokens: bfloat16 [8, 8192, 2560], P('section', 'expert'), may hold values from -6 to 6
- routes: int32 [8, 8192, 6], P('section', 'expert'), may hold values from 0 to 159, all different within a row
- route_weights: float32 [8, 8192, 6], P('section', 'expert'), may hold values from 0.05 to 1
- cotangent: bfloat16 [8, 8192, 2560], P('section', 'expert'), may hold values from -6 to 6
- w_gate: bfloat16 [8, 2560, 8192], P('section', None, 'expert'), as said below
- w_up: bfloat16 [8, 2560, 8192], P('section', None, 'expert'), as said below
- w_down: bfloat16 [8, 8192, 2560], P('section', 'expert'), as said below
Outputs:
- mixed: bfloat16 [8, 8192, 2560], P('section', 'expert')
- grad_tokens: bfloat16 [8, 8192, 2560], P('section', 'expert')
- grad_gate: bfloat16 [8, 2560, 8192], P('section', None, 'expert')
- grad_up: bfloat16 [8, 2560, 8192], P('section', None, 'expert')
- grad_down: bfloat16 [8, 8192, 2560], P('section', 'expert')
The draws below stay inside these ranges and needn't reach their ends.
Inputs may be any that keep to these rules, and one draw needn't show every extreme that they name: w_gate[g] equals w_gate[7 - g] for every g. w_up[g] equals w_up[7 - g] for every g. w_down[g] equals w_down[7 - g] for every g.
All inputs are finite; a program needn't handle non-finite values.
Results may differ from the reference program's by a relative error of at most 0.0065.
Values may be sent and summed in bfloat16 or wider, within the bound.
A program may use at most 128 MiB of HBM per device.

```python
import math
import jax
import jax.numpy as jnp
from jax import lax

D = 2560
EXP_HID = 1024
EXPERTS = 160
TOP = 6
SPLIT = 4
TOK_DEV = 256
CAP = 16
HID_DEV = 256
EXP_WIN = 8
EXP_COLS = 8192
TOK_GROUP = 8192
N_SECTION = 8
N_EXPERT = 32


def mirrored(key, height, width, factor):
    half = jax.random.normal(key, (N_SECTION // 2, height, width), jnp.float32) * factor
    return jnp.concatenate([half, half[::-1]], axis=0).astype(jnp.bfloat16)


def draw_w_gate(key, part):
    key = jax.random.fold_in(key, 11)
    return mirrored(key, D, EXP_COLS, D ** (-0.5))


def draw_w_up(key, part):
    key = jax.random.fold_in(key, 12)
    return mirrored(key, D, EXP_COLS, D ** (-0.5))


def draw_w_down(key, part):
    key = jax.random.fold_in(key, 13)
    return mirrored(key, EXP_COLS, D, EXP_HID ** (-0.5))


def levels(key, dims, shards, low, top_value):
    gain = 1.0
    for axis_at, blocks in shards:
        steps = jax.random.uniform(jax.random.fold_in(jax.random.fold_in(key, 6), axis_at), (blocks,), jnp.float32, low / len(shards), top_value / len(shards))
        gain = gain * jnp.repeat(jnp.exp(steps), dims[axis_at] // blocks).reshape((-1,) + (1,) * (len(dims) - 1 - axis_at))
    return gain


def different_ones(own_key, rows, amount, top, lift):
    order = jax.random.permutation(jax.random.fold_in(own_key, 1), amount)
    pull = order
    for power in range(3):
        pull = pull * pull // amount
    pull = pull * lift // amount
    lots = jax.random.randint(jax.random.fold_in(own_key, 2), (rows, amount), 0, 4096) + pull
    sure = jax.random.permutation(jax.random.fold_in(own_key, 3), rows)[jnp.arange(amount) % rows]
    lots = jnp.where(jnp.arange(rows)[:, None] == sure[None, :], 1 << 14, lots)
    merit = lots * amount + jnp.arange(amount)
    return lax.top_k(merit.astype(jnp.int32), top)[1].astype(jnp.int32)


def centred(own_key, shape, scale, reach, pieces=(), kind=jnp.bfloat16):
    level = levels(own_key, shape, pieces, -0.22, 0.18) if pieces else 1.0
    values = jax.random.normal(own_key, shape, jnp.float32) * scale * level
    return jnp.minimum(jnp.maximum(values, -reach), reach).astype(kind)


def setup_inputs(seed: int = 0) -> dict:
    arg_keys = jax.random.split(jax.random.key(seed), 8)
    tokens = centred(arg_keys[0], (N_SECTION, TOK_GROUP, D), 1.0, 6.0, ((0, 8), (1, 32)))
    routes = different_ones(arg_keys[1], N_SECTION * TOK_GROUP, EXPERTS, TOP, 614).reshape((N_SECTION, TOK_GROUP, TOP))
    route_weights = jnp.clip(jnp.exp(math.log(1.0) - 2.9957323 * jax.random.uniform(arg_keys[2], (N_SECTION, TOK_GROUP, TOP), jnp.float32) ** levels(arg_keys[2], (N_SECTION, TOK_GROUP, TOP), ((0, 8), (1, 32)), -0.2, 0.2)), 0.05, 1.0)
    cotangent = centred(arg_keys[3], (N_SECTION, TOK_GROUP, D), 1.0, 6.0, ((0, 8), (1, 32)))
    w_gate = draw_w_gate(jax.random.fold_in(arg_keys[7], 71), 0)
    w_up = draw_w_up(jax.random.fold_in(arg_keys[7], 71), 0)
    w_down = draw_w_down(jax.random.fold_in(arg_keys[7], 71), 0)
    return {"tokens": tokens, "routes": routes, "route_weights": route_weights, "cotangent": cotangent, "w_gate": w_gate, "w_up": w_up, "w_down": w_down}


def rounded(value):
    return lax.optimization_barrier(value.astype(jnp.bfloat16)).astype(jnp.float32)


def group_pass(tokens, routes, route_weights, cotangent, w_gate, w_up, w_down):
    count = tokens.shape[0]
    window = jnp.arange(EXP_WIN, dtype=jnp.int32)
    onehot = routes[:, :, None] == window[None, None, :]
    hits = jnp.sum(onehot.astype(jnp.int32), axis=1)
    weight = jnp.sum(jnp.where(onehot, route_weights[:, :, None], jnp.zeros((), route_weights.dtype)), axis=1)
    blocks = hits.reshape(N_EXPERT, TOK_DEV, EXP_WIN)
    slot = (jnp.cumsum(blocks, axis=1) - blocks).reshape(count, EXP_WIN)
    kept = (hits > 0) & (slot < CAP)
    source = jnp.arange(count, dtype=jnp.int32) // TOK_DEV
    rows_all = N_EXPERT * CAP
    mixed = jnp.zeros((count, D), jnp.float32)
    grad_in = jnp.zeros((count, D), jnp.float32)
    grads_gate, grads_up, grads_down = [], [], []
    for expert in range(EXP_WIN):
        target = jnp.where(kept[:, expert], source * CAP + slot[:, expert], rows_all).astype(jnp.int32)
        rows = jnp.zeros((rows_all, D), jnp.bfloat16).at[target].set(tokens, mode="drop")
        scaled = (weight[:, expert:expert + 1] * cotangent.astype(jnp.float32)).astype(jnp.bfloat16)
        grad_rows = jnp.zeros((rows_all, D), jnp.bfloat16).at[target].set(scaled, mode="drop")
        lower = expert * EXP_HID
        gate_cols = w_gate[:, lower:lower + EXP_HID]
        up_cols = w_up[:, lower:lower + EXP_HID]
        down_rows = w_down[lower:lower + EXP_HID, :]
        gate = jnp.dot(rows, gate_cols, preferred_element_type=jnp.float32)
        up = jnp.dot(rows, up_cols, preferred_element_type=jnp.float32)
        sig = jax.nn.sigmoid(gate)
        hidden = (gate * sig * up).astype(jnp.bfloat16)
        dh = jnp.dot(grad_rows, down_rows.T, preferred_element_type=jnp.float32)
        dgate = (dh * up * sig * (1.0 + gate * (1.0 - sig))).astype(jnp.bfloat16)
        dup = (dh * gate * sig).astype(jnp.bfloat16)
        out = jnp.zeros((rows_all, D), jnp.float32)
        back = jnp.zeros((rows_all, D), jnp.float32)
        for quarter in range(SPLIT):
            low = quarter * HID_DEV
            high = low + HID_DEV
            out = out + rounded(jnp.dot(hidden[:, low:high], down_rows[low:high], preferred_element_type=jnp.float32))
            piece = jnp.dot(dgate[:, low:high], gate_cols[:, low:high].T, preferred_element_type=jnp.float32)
            piece = piece + jnp.dot(dup[:, low:high], up_cols[:, low:high].T, preferred_element_type=jnp.float32)
            back = back + rounded(piece)
        picked = jnp.minimum(target, rows_all - 1)
        live = kept[:, expert].astype(jnp.float32)[:, None]
        mixed = mixed + (live * weight[:, expert:expert + 1]) * out[picked]
        grads_gate.append(jnp.dot(rows.T, dgate, preferred_element_type=jnp.float32).astype(jnp.bfloat16))
        grads_up.append(jnp.dot(rows.T, dup, preferred_element_type=jnp.float32).astype(jnp.bfloat16))
        grads_down.append(jnp.dot(hidden.T, grad_rows, preferred_element_type=jnp.float32).astype(jnp.bfloat16))
        grad_in = grad_in + live * back[picked]
    return (mixed.astype(jnp.bfloat16), grad_in.astype(jnp.bfloat16),
            jnp.concatenate(grads_gate, axis=1), jnp.concatenate(grads_up, axis=1),
            jnp.concatenate(grads_down, axis=0))


def mirror_sum(stacked):
    return (stacked.astype(jnp.float32) + stacked[::-1].astype(jnp.float32)).astype(jnp.bfloat16)


def reference(tokens, routes, route_weights, cotangent, w_gate, w_up, w_down):
    outputs = []
    for group in range(N_SECTION):
        outputs.append(group_pass(tokens[group], routes[group], route_weights[group], cotangent[group],
                                  w_gate[group], w_up[group], w_down[group]))
    mixed = jnp.stack([item[0] for item in outputs])
    grad_tokens = jnp.stack([item[1] for item in outputs])
    grad_gate = mirror_sum(jnp.stack([item[2] for item in outputs]))
    grad_up = mirror_sum(jnp.stack([item[3] for item in outputs]))
    grad_down = mirror_sum(jnp.stack([item[4] for item in outputs]))
    return (mixed, grad_tokens, grad_gate, grad_up, grad_down)
```

```python
import functools

import jax
import jax.numpy as jnp
from jax import lax
from jax.experimental import pallas as pl
from jax.experimental.pallas import tpu as pltpu
from jax.sharding import PartitionSpec as P

SPLIT = 4
CAP = 16
MESH = pl.DeviceIdType.MESH
F32 = jnp.float32
BF16 = jnp.bfloat16

OWN, RIGHT, LEFT, OPPOSITE = range(4)


def nt(left, right):
    return lax.dot_general(left, right, (((1,), (1,)), ((), ())), preferred_element_type=F32)


def tn(left, right):
    return lax.dot_general(left, right, (((0,), (0,)), ((), ())), preferred_element_type=F32)


def nn(left, right):
    return jnp.dot(left, right, preferred_element_type=F32)


def kernel(
    n_section, window, step,
    tokens, routes, route_weights, cotangent, gate_hbm, up_hbm, down_hbm,
    mixed, grad_in, grad_gate, grad_up, grad_down,
    w_gate, w_up, w_down, send, held, weights_hi, weights_lo, chosen,
    gate_val, up_val, act, part, via, last, ret_send, ret,
    sum_gate, sum_up, sum_down,
    w_sem, a_send, a_recv, y_send, y_recv, r_send, r_recv, e_send, e_recv,
):
    group = lax.axis_index("section")
    index = lax.axis_index("expert")
    expert = index // SPLIT
    quarter = index % SPLIT
    mirror = n_section - 1 - group
    shard = window * CAP
    half = shard // 2
    n_tok, width = tokens.shape

    right = (group, expert * SPLIT + (quarter + 1) % SPLIT)
    left = (group, expert * SPLIT + (quarter + SPLIT - 1) % SPLIT)

    def at_expert(g, j):
        return (g, (expert + j) % window * SPLIT + quarter)

    weight_copies = [
        pltpu.make_async_copy(src, dst, w_sem.at[i])
        for i, (src, dst) in enumerate(((gate_hbm, w_gate), (up_hbm, w_up), (down_hbm, w_down)))
    ]
    for copy in weight_copies:
        copy.start()

    barrier = pltpu.get_barrier_semaphore()
    friends = [right, left]
    friends += [at_expert(group, j) for j in range(1, window)]
    friends += [at_expert(mirror, j) for j in range(window)]
    for friend in friends:
        pl.semaphore_signal(barrier, inc=1, device_id=friend, device_id_type=MESH)

    def remote(src, dst, send_sem, recv_sem, device):
        pltpu.make_async_remote_copy(
            src_ref=src, dst_ref=dst, send_sem=send_sem, recv_sem=recv_sem,
            device_id=device, device_id_type=MESH,
        ).start()

    def settle(ref, sem):
        pltpu.make_async_copy(ref, ref, sem).wait()

    def chunks(body, total=width):
        def run(i, carry):
            body(pl.ds(pl.multiple_of(i * step, step), step))
            return carry

        lax.fori_loop(0, total // step, run, 0)

    column = lax.broadcasted_iota(jnp.int32, (n_tok, shard), 1)
    wanted = (expert + column // CAP) % window
    hits = jnp.zeros((n_tok, shard), F32)
    weight = jnp.zeros((n_tok, shard), F32)
    for k in range(routes.shape[1]):
        same = routes[:, k : k + 1] == wanted
        hits = jnp.where(same, 1.0, hits)
        weight = weight + jnp.where(same, route_weights[:, k : k + 1], 0.0)
    before = lax.broadcasted_iota(jnp.int32, (n_tok, n_tok), 0) > lax.broadcasted_iota(
        jnp.int32, (n_tok, n_tok), 1
    )
    slot = nn(jnp.where(before, 1.0, 0.0).astype(BF16), hits.astype(BF16))
    kept = (hits > 0.0) & (slot == (column % CAP).astype(F32))
    select = jnp.where(kept, 1.0, 0.0)
    weight = jnp.where(kept, weight, 0.0)
    high = weight.astype(BF16)
    weights_hi[...] = high
    weights_lo[...] = (weight - high.astype(F32)).astype(BF16)
    chosen[...] = select.astype(BF16)
    select_t = jnp.transpose(select).astype(BF16)
    scale = jnp.sum(jnp.transpose(weight), axis=1, keepdims=True)

    def pick_rows(at):
        send[0, :, at] = nn(select_t, tokens[:, at]).astype(BF16)
        held[0, 0, :CAP, at] = send[0, :CAP, at]

    def pick_scaled(at):
        send[1, :, at] = (scale * nn(select_t, cotangent[:, at])).astype(BF16)
        held[1, 0, :CAP, at] = send[1, :CAP, at]

    def block(j):
        return pl.ds(j * CAP, CAP)

    def dispatch(t, k):
        g = (group, mirror)[k]
        for j in range(1 - k, window):
            remote(
                send.at[t, block(j)], held.at[t, k, block(j)],
                a_send.at[t, k], a_recv.at[t, k, j // (window // 2)], at_expert(g, j),
            )

    def rows_of(which, h=None):
        if h is None:
            return pl.ds(which * shard, shard)
        return pl.ds(which * shard + h * half, half)

    def gather(t, k):
        for h in range(2):
            skip = CAP if k == 0 and h == 0 else 0
            settle(held.at[t, k, pl.ds(h * half + skip, half - skip)], a_recv.at[t, k, h])
            mine = held.at[t, k, rows_of(OWN, h)]
            remote(mine, held.at[t, k, rows_of(LEFT, h)], y_send.at[t, k, h], y_recv.at[t, k, h], right)
            remote(mine, held.at[t, k, rows_of(RIGHT, h)], y_send.at[t, k, 2 + h], y_recv.at[t, k, 2 + h], left)

    def forward(t, k):
        from_left = [(held.at[t, k, rows_of(LEFT, h)], y_recv.at[t, k, h]) for h in range(2)]
        from_right = [(held.at[t, k, rows_of(RIGHT, h)], y_recv.at[t, k, 2 + h]) for h in range(2)]
        settle(*from_right[0])
        remote(from_right[0][0], held.at[t, k, rows_of(OPPOSITE, 0)], y_send.at[t, k, 4], y_recv.at[t, k, 4], left)
        settle(*from_left[0])
        settle(*from_left[1])
        remote(from_left[1][0], held.at[t, k, rows_of(OPPOSITE, 1)], y_send.at[t, k, 5], y_recv.at[t, k, 5], right)
        settle(*from_right[1])

    def far(t, k):
        for h in range(2):
            settle(held.at[t, k, rows_of(OPPOSITE, h)], y_recv.at[t, k, 4 + h])

    def forward_pass(k, first, count):
        rows = pl.ds(first * shard, count * shard)
        x = held[0, k, rows]
        gate_val[rows] = nn(x, w_gate[...])
        up_val[rows] = nn(x, w_up[...])

    def backward_pass(k, first, count):
        rows = pl.ds(first * shard, count * shard)
        dh = nt(held[1, k, rows], w_down[...])
        gate, up = gate_val[rows], up_val[rows]
        sig = jax.nn.sigmoid(gate)
        act[0, k, rows] = (gate * sig * up).astype(BF16)
        act[1, k, rows] = (dh * up * sig * (1.0 + gate * (1.0 - sig))).astype(BF16)
        act[2, k, rows] = (dh * gate * sig).astype(BF16)

    def parts(first, count):
        rows = pl.ds(first * shard, count * shard)

        def one(at):
            part[0, rows, at] = nn(act[0, 0, rows], w_down[:, at]).astype(BF16)
            part[1, rows, at] = (
                nt(act[1, 0, rows], w_gate[at, :]) + nt(act[2, 0, rows], w_up[at, :])
            ).astype(BF16)

        chunks(one)

    def gradients(k, first, count, start, stop):
        rows = pl.ds(first * shard, count * shard)

        def one(at):
            x, g = held[0, k, rows, at], held[1, k, rows, at]
            terms = (tn(x, act[1, k, rows]), tn(x, act[2, k, rows]), tn(act[0, k, rows], g))
            where = ((at, slice(None)), (at, slice(None)), (slice(None), at))
            for total, out, term, place in zip((sum_gate, sum_up, sum_down), (grad_gate, grad_up, grad_down), terms, where):
                if not start:
                    term = total[place] + term
                if stop:
                    out[place] = term.astype(BF16)
                else:
                    total[place] = term

        chunks(one)

    chunks(pick_rows)
    pl.semaphore_wait(barrier, len(friends))
    dispatch(0, 0)
    chunks(pick_scaled)
    dispatch(1, 0)
    dispatch(0, 1)
    dispatch(1, 1)

    gather(0, 0)
    for copy in weight_copies:
        copy.wait()
    forward_pass(0, OWN, 1)
    gather(1, 0)
    backward_pass(0, OWN, 1)
    parts(OWN, 1)
    forward(0, 0)
    forward_pass(0, RIGHT, 2)
    forward(1, 0)
    backward_pass(0, RIGHT, 2)
    parts(RIGHT, 2)

    for t in range(2):
        remote(part.at[t, rows_of(RIGHT, 1)], last.at[t, rows_of(0, 1)], r_send.at[t, 3], r_recv.at[t, 3], right)
        remote(part.at[t, rows_of(LEFT, 0)], last.at[t, rows_of(1, 0)], r_send.at[t, 4], r_recv.at[t, 4], left)
    far(0, 0)
    forward_pass(0, OPPOSITE, 1)
    far(1, 0)
    backward_pass(0, OPPOSITE, 1)
    parts(OPPOSITE, 1)
    for t in range(2):
        remote(part.at[t, rows_of(OPPOSITE, 0)], via.at[t, 0], r_send.at[t, 0], r_recv.at[t, 0], right)
        remote(part.at[t, rows_of(OPPOSITE, 1)], via.at[t, 1], r_send.at[t, 1], r_recv.at[t, 1], left)
    gather(0, 1)
    gradients(0, OWN, 4, True, False)

    for t in range(2):
        settle(via.at[t, 0], r_recv.at[t, 0])
        rows = rows_of(RIGHT, 0)
        part[t, rows] = (part[t, rows].astype(F32) + via[t, 0].astype(F32)).astype(BF16)
        remote(part.at[t, rows], last.at[t, rows_of(0, 0)], r_send.at[t, 2], r_recv.at[t, 2], right)
        settle(via.at[t, 1], r_recv.at[t, 1])
        rows = rows_of(LEFT, 1)
        part[t, rows] = (part[t, rows].astype(F32) + via[t, 1].astype(F32)).astype(BF16)
        remote(part.at[t, rows], last.at[t, rows_of(1, 1)], r_send.at[t, 5], r_recv.at[t, 5], left)

    forward(0, 1)
    gather(1, 1)
    forward_pass(1, OWN, 3)

    for t in range(2):
        for h in range(2):
            settle(last.at[t, rows_of(0, h)], r_recv.at[t, 2 + h])
            settle(last.at[t, rows_of(1, h)], r_recv.at[t, 4 + h])
            rows = rows_of(OWN, h)
            total = part[t, rows].astype(F32) + last[t, rows_of(0, h)].astype(F32) + last[t, rows_of(1, h)].astype(F32)
            ret_send[t, rows] = total.astype(BF16)
        ret[t, :CAP] = ret_send[t, :CAP]
        for j in range(1, window):
            remote(
                ret_send.at[t, block(j)], ret.at[t, block(j)],
                e_send.at[t], e_recv.at[t], at_expert(group, window - j),
            )

    forward(1, 1)
    backward_pass(1, OWN, 3)
    far(0, 1)
    forward_pass(1, OPPOSITE, 1)
    gradients(1, OWN, 3, False, False)

    rest = pl.ds(CAP, shard - CAP)
    settle(ret.at[0, rest], e_recv.at[0])

    def combine_out(at):
        mixed[:, at] = (nn(weights_hi[...], ret[0, :, at]) + nn(weights_lo[...], ret[0, :, at])).astype(BF16)

    chunks(combine_out)
    settle(ret.at[1, rest], e_recv.at[1])

    def combine_back(at):
        grad_in[:, at] = nn(chosen[...], ret[1, :, at]).astype(BF16)

    chunks(combine_back)

    far(1, 1)
    backward_pass(1, OPPOSITE, 1)
    gradients(1, OPPOSITE, 1, False, True)

    for t in range(2):
        for k in range(2):
            left_out = CAP if k == 0 else 0
            settle(send.at[t, pl.ds(left_out, shard - left_out)], a_send.at[t, k])
            for i in range(6):
                settle(held.at[t, k, rows_of(OWN, 0)], y_send.at[t, k, i])
        for i in range(6):
            settle(via.at[t, 0], r_send.at[t, i])
        settle(ret_send.at[t, rest], e_send.at[t])


def solution(mesh):
    n_section = mesh.shape["section"]
    window = mesh.shape["expert"] // SPLIT

    def per_device(tokens, routes, route_weights, cotangent, w_gate, w_up, w_down):
        _, n_tok, width = tokens.shape
        hidden = w_gate.shape[2]
        shard = window * CAP
        rows = SPLIT * shard
        step = 512 if width % 512 == 0 else 128
        vmem = pl.BlockSpec(memory_space=pltpu.VMEM)
        hbm = pl.BlockSpec(memory_space=pl.ANY)
        dma = pltpu.SemaphoreType.DMA
        flops = 2 * rows * width * hidden * 15
        outs = pl.pallas_call(
            functools.partial(kernel, n_section, window, step),
            out_shape=(
                jax.ShapeDtypeStruct((n_tok, width), BF16),
                jax.ShapeDtypeStruct((n_tok, width), BF16),
                jax.ShapeDtypeStruct((width, hidden), BF16),
                jax.ShapeDtypeStruct((width, hidden), BF16),
                jax.ShapeDtypeStruct((hidden, width), BF16),
            ),
            in_specs=[vmem] * 4 + [hbm] * 3,
            out_specs=(vmem,) * 5,
            scratch_shapes=[
                pltpu.VMEM((width, hidden), BF16),
                pltpu.VMEM((width, hidden), BF16),
                pltpu.VMEM((hidden, width), BF16),
                pltpu.VMEM((2, shard, width), BF16),
                pltpu.VMEM((2, 2, rows, width), BF16),
                pltpu.VMEM((n_tok, shard), BF16),
                pltpu.VMEM((n_tok, shard), BF16),
                pltpu.VMEM((n_tok, shard), BF16),
                pltpu.VMEM((rows, hidden), F32),
                pltpu.VMEM((rows, hidden), F32),
                pltpu.VMEM((3, 2, rows, hidden), BF16),
                pltpu.VMEM((2, rows, width), BF16),
                pltpu.VMEM((2, 2, shard // 2, width), BF16),
                pltpu.VMEM((2, 2 * shard, width), BF16),
                pltpu.VMEM((2, shard, width), BF16),
                pltpu.VMEM((2, shard, width), BF16),
                pltpu.VMEM((width, hidden), F32),
                pltpu.VMEM((width, hidden), F32),
                pltpu.VMEM((hidden, width), F32),
                dma((3,)),
                dma((2, 2)),
                dma((2, 2, 2)),
                dma((2, 2, 6)),
                dma((2, 2, 6)),
                dma((2, 6)),
                dma((2, 6)),
                dma((2,)),
                dma((2,)),
            ],
            compiler_params=pltpu.CompilerParams(
                collective_id=0, has_side_effects=True, vmem_limit_bytes=60 * 2**20
            ),
            cost_estimate=pl.CostEstimate(flops=flops, bytes_accessed=2 * 8 * n_tok * width, transcendentals=0),
        )(tokens[0], routes[0], route_weights[0], cotangent[0], w_gate[0], w_up[0], w_down[0])
        return tuple(out[None] for out in outs)

    return jax.shard_map(
        per_device,
        mesh=mesh,
        in_specs=(
            P("section", "expert", None),
            P("section", "expert", None),
            P("section", "expert", None),
            P("section", "expert", None),
            P("section", None, "expert"),
            P("section", None, "expert"),
            P("section", "expert", None),
        ),
        out_specs=(
            P("section", "expert", None),
            P("section", "expert", None),
            P("section", None, "expert"),
            P("section", None, "expert"),
            P("section", "expert", None),
        ),
        check_vma=False,
    )
```

```python
import functools

import jax
import jax.numpy as jnp
from jax import lax
from jax.experimental import pallas as pl
from jax.experimental.pallas import tpu as pltpu
from jax.sharding import PartitionSpec as P

SPLIT = 4
CAP = 16
MESH = pl.DeviceIdType.MESH
F32 = jnp.float32
BF16 = jnp.bfloat16

OWN, RIGHT, LEFT, OPPOSITE = range(4)
ACROSS = ((0, 0), (0, 1))


def nt(left, right):
    return lax.dot_general(left, right, (((1,), (1,)), ((), ())), preferred_element_type=F32)


def tn(left, right):
    return lax.dot_general(left, right, (((0,), (0,)), ((), ())), preferred_element_type=F32)


def nn(left, right):
    return jnp.dot(left, right, preferred_element_type=F32)


def kernel(
    n_section, window, step,
    tokens_hbm, routes, route_weights, cotangent_hbm, gate_hbm, up_hbm, down_hbm,
    mixed_hbm, grad_in_hbm, grad_gate_hbm, grad_up_hbm, grad_down_hbm,
    tokens, cotangent, w_gate, w_up, w_down, send, held, weights_hi, weights_lo, chosen,
    gate_val, up_val, act, part, via, last, ret_send, ret,
    sum_gate, sum_up, sum_down,
    in_sem, out_sem, a_send, a_recv, y_send, y_recv, r_send, r_recv, e_send, e_recv,
):
    group = lax.axis_index("section")
    index = lax.axis_index("expert")
    expert = index // SPLIT
    quarter = index % SPLIT
    mirror = n_section - 1 - group
    shard = window * CAP
    half = shard // 2
    n_tok, width = tokens.shape

    right = (group, expert * SPLIT + (quarter + 1) % SPLIT)
    left = (group, expert * SPLIT + (quarter + SPLIT - 1) % SPLIT)

    def at_expert(g, j):
        return (g, (expert + j) % window * SPLIT + quarter)

    sources = (tokens_hbm, cotangent_hbm, gate_hbm, up_hbm, down_hbm)
    places = (tokens, cotangent, w_gate, w_up, w_down)
    loads = [pltpu.make_async_copy(src, dst, in_sem.at[i]) for i, (src, dst) in enumerate(zip(sources, places))]
    results = (mixed_hbm, grad_in_hbm, grad_gate_hbm, grad_up_hbm, grad_down_hbm)
    stores = [pltpu.make_async_copy(src, dst, out_sem.at[i]) for i, (src, dst) in enumerate(zip(places, results))]
    for copy in loads[:2]:
        copy.start()

    barrier = pltpu.get_barrier_semaphore()
    friends = [right, left]
    friends += [at_expert(group, j) for j in range(1, window)]
    friends += [at_expert(mirror, j) for j in range(window)]
    for friend in friends:
        pl.semaphore_signal(barrier, inc=1, device_id=friend, device_id_type=MESH)

    def remote(src, dst, send_sem, recv_sem, device):
        pltpu.make_async_remote_copy(
            src_ref=src, dst_ref=dst, send_sem=send_sem, recv_sem=recv_sem,
            device_id=device, device_id_type=MESH,
        ).start()

    def settle(ref, sem):
        pltpu.make_async_copy(ref, ref, sem).wait()

    def chunks(body, total=width):
        def run(i, carry):
            body(pl.ds(pl.multiple_of(i * step, step), step))
            return carry

        lax.fori_loop(0, total // step, run, 0)

    row = lax.broadcasted_iota(jnp.int32, (shard, n_tok), 0)
    wanted = (expert + row // CAP) % window
    hits = jnp.zeros((shard, n_tok), F32)
    weight = jnp.zeros((shard, n_tok), F32)
    for k in range(routes.shape[0]):
        same = routes[k : k + 1] == wanted
        hits = jnp.where(same, 1.0, hits)
        weight = weight + jnp.where(same, route_weights[k : k + 1], 0.0)
    before = lax.broadcasted_iota(jnp.int32, (n_tok, n_tok), 0) < lax.broadcasted_iota(
        jnp.int32, (n_tok, n_tok), 1
    )
    slot = nn(hits.astype(BF16), jnp.where(before, 1.0, 0.0).astype(BF16))
    kept = (hits > 0.0) & (slot == (row % CAP).astype(F32))
    select = jnp.where(kept, 1.0, 0.0)
    weight = jnp.where(kept, weight, 0.0)
    select_t = select.astype(BF16)
    scale = jnp.sum(weight, axis=1, keepdims=True)

    def pick_rows(at):
        send[0, :, at] = nn(select_t, tokens[:, at]).astype(BF16)
        held[0, 0, :CAP, at] = send[0, :CAP, at]

    def pick_scaled(at):
        send[1, :, at] = (scale * nn(select_t, cotangent[:, at])).astype(BF16)
        held[1, 0, :CAP, at] = send[1, :CAP, at]

    def block(j):
        return pl.ds(j * CAP, CAP)

    def dispatch(t, k):
        g = (group, mirror)[k]
        for j in range(1 - k, window):
            remote(
                send.at[t, block(j)], held.at[t, k, block(j)],
                a_send.at[t, k], a_recv.at[t, k, j // (window // 2)], at_expert(g, j),
            )

    def rows_of(which, h=None):
        if h is None:
            return pl.ds(which * shard, shard)
        return pl.ds(which * shard + h * half, half)

    def both_ways(t, k, h, low, count):
        def part_of(which):
            return held.at[t, k, pl.ds(which * shard + h * half + low, count)]

        remote(part_of(OWN), part_of(LEFT), y_send.at[t, k, h], y_recv.at[t, k, h], right)
        remote(part_of(OWN), part_of(RIGHT), y_send.at[t, k, 2 + h], y_recv.at[t, k, 2 + h], left)

    def gather(t, k):
        for h in range(2):
            skip = CAP if k == 0 and h == 0 else 0
            settle(held.at[t, k, pl.ds(h * half + skip, half - skip)], a_recv.at[t, k, h])
            both_ways(t, k, h, skip, half - skip)

    def forward(t, k):
        from_left = [(held.at[t, k, rows_of(LEFT, h)], y_recv.at[t, k, h]) for h in range(2)]
        from_right = [(held.at[t, k, rows_of(RIGHT, h)], y_recv.at[t, k, 2 + h]) for h in range(2)]
        settle(*from_right[0])
        if k == 0 or (t, 0) not in ACROSS:
            remote(from_right[0][0], held.at[t, k, rows_of(OPPOSITE, 0)], y_send.at[t, k, 4], y_recv.at[t, k, 4], left)
        settle(*from_left[0])
        settle(*from_left[1])
        if k == 0 or (t, 1) not in ACROSS:
            remote(from_left[1][0], held.at[t, k, rows_of(OPPOSITE, 1)], y_send.at[t, k, 5], y_recv.at[t, k, 5], right)
        settle(*from_right[1])

    def far(t, k):
        for h in range(2):
            shard_half = held.at[t, k, rows_of(OPPOSITE, h)]
            settle(shard_half, y_recv.at[t, k, 4 + h])
            if k == 0 and (t, h) in ACROSS:
                remote(
                    shard_half, held.at[t, 1, rows_of(OPPOSITE, h)],
                    y_send.at[t, 1, 4 + h], y_recv.at[t, 1, 4 + h], at_expert(mirror, 0),
                )

    def forward_pass(k, first, count):
        rows = pl.ds(first * shard, count * shard)
        x = held[0, k, rows]
        gate_val[rows] = nn(x, w_gate[...])
        up_val[rows] = nn(x, w_up[...])

    def backward_pass(k, first, count):
        rows = pl.ds(first * shard, count * shard)
        dh = nt(held[1, k, rows], w_down[...])
        gate, up = gate_val[rows], up_val[rows]
        sig = jax.nn.sigmoid(gate)
        act[0, k, rows] = (gate * sig * up).astype(BF16)
        act[1, k, rows] = (dh * up * sig * (1.0 + gate * (1.0 - sig))).astype(BF16)
        act[2, k, rows] = (dh * gate * sig).astype(BF16)

    def parts(first, count):
        rows = pl.ds(first * shard, count * shard)

        def one(at):
            part[0, rows, at] = nn(act[0, 0, rows], w_down[:, at]).astype(BF16)
            part[1, rows, at] = (
                nt(act[1, 0, rows], w_gate[at, :]) + nt(act[2, 0, rows], w_up[at, :])
            ).astype(BF16)

        chunks(one)

    def gradients(k, first, count, start, stop):
        rows = pl.ds(first * shard, count * shard)

        def one(at):
            x, g = held[0, k, rows, at], held[1, k, rows, at]
            terms = (tn(x, act[1, k, rows]), tn(x, act[2, k, rows]), tn(act[0, k, rows], g))
            where = ((at, slice(None)), (at, slice(None)), (slice(None), at))
            for total, out, term, place in zip((sum_gate, sum_up, sum_down), places[2:], terms, where):
                if not start:
                    term = total[place] + term
                if stop:
                    out[place] = term.astype(BF16)
                else:
                    total[place] = term

        chunks(one)

    loads[0].wait()
    chunks(pick_rows)
    pl.semaphore_wait(barrier, len(friends))
    dispatch(0, 0)
    both_ways(0, 0, 0, 0, CAP)
    loads[1].wait()
    chunks(pick_scaled)
    dispatch(1, 0)
    both_ways(1, 0, 0, 0, CAP)
    for copy in loads[2:]:
        copy.start()
    weight_t = jnp.transpose(weight)
    high = weight_t.astype(BF16)
    weights_hi[...] = high
    weights_lo[...] = (weight_t - high.astype(F32)).astype(BF16)
    chosen[...] = jnp.transpose(select).astype(BF16)

    gather(0, 0)
    dispatch(0, 1)
    gather(1, 0)
    dispatch(1, 1)
    for copy in loads[2:]:
        copy.wait()
    forward_pass(0, OWN, 1)
    forward(0, 0)
    backward_pass(0, OWN, 1)
    parts(OWN, 1)
    forward_pass(0, RIGHT, 2)
    forward(1, 0)
    far(0, 0)
    backward_pass(0, RIGHT, 2)
    parts(RIGHT, 2)

    for t in range(2):
        remote(part.at[t, rows_of(RIGHT, 1)], last.at[t, rows_of(0, 1)], r_send.at[t, 3], r_recv.at[t, 3], right)
        remote(part.at[t, rows_of(LEFT, 0)], last.at[t, rows_of(1, 0)], r_send.at[t, 4], r_recv.at[t, 4], left)
    forward_pass(0, OPPOSITE, 1)
    far(1, 0)
    backward_pass(0, OPPOSITE, 1)
    parts(OPPOSITE, 1)
    for t in range(2):
        remote(part.at[t, rows_of(OPPOSITE, 0)], via.at[t, 0], r_send.at[t, 0], r_recv.at[t, 0], right)
        remote(part.at[t, rows_of(OPPOSITE, 1)], via.at[t, 1], r_send.at[t, 1], r_recv.at[t, 1], left)
    gather(0, 1)
    forward_pass(1, OWN, 1)

    for t in range(2):
        settle(via.at[t, 0], r_recv.at[t, 0])
        rows = rows_of(RIGHT, 0)
        part[t, rows] = (part[t, rows].astype(F32) + via[t, 0].astype(F32)).astype(BF16)
        remote(part.at[t, rows], last.at[t, rows_of(0, 0)], r_send.at[t, 2], r_recv.at[t, 2], right)
        settle(via.at[t, 1], r_recv.at[t, 1])
        rows = rows_of(LEFT, 1)
        part[t, rows] = (part[t, rows].astype(F32) + via[t, 1].astype(F32)).astype(BF16)
        remote(part.at[t, rows], last.at[t, rows_of(1, 1)], r_send.at[t, 5], r_recv.at[t, 5], left)

    gather(1, 1)
    gradients(0, OWN, 4, True, False)

    for t in range(2):
        for h in range(2):
            settle(last.at[t, rows_of(0, h)], r_recv.at[t, 2 + h])
            settle(last.at[t, rows_of(1, h)], r_recv.at[t, 4 + h])
            rows = rows_of(OWN, h)
            total = part[t, rows].astype(F32) + last[t, rows_of(0, h)].astype(F32) + last[t, rows_of(1, h)].astype(F32)
            ret_send[t, rows] = total.astype(BF16)
        ret[t, :CAP] = ret_send[t, :CAP]
        for j in range(1, window):
            remote(
                ret_send.at[t, block(j)], ret.at[t, block(j)],
                e_send.at[t], e_recv.at[t], at_expert(group, window - j),
            )

    backward_pass(1, OWN, 1)
    gradients(1, OWN, 1, False, False)
    forward(0, 1)
    forward_pass(1, RIGHT, 2)
    far(0, 1)
    forward_pass(1, OPPOSITE, 1)

    rest = pl.ds(CAP, shard - CAP)
    settle(ret.at[0, rest], e_recv.at[0])

    def combine_out(at):
        tokens[:, at] = (nn(weights_hi[...], ret[0, :, at]) + nn(weights_lo[...], ret[0, :, at])).astype(BF16)

    chunks(combine_out)
    stores[0].start()
    settle(ret.at[1, rest], e_recv.at[1])

    def combine_back(at):
        cotangent[:, at] = nn(chosen[...], ret[1, :, at]).astype(BF16)

    chunks(combine_back)
    stores[1].start()

    forward(1, 1)
    backward_pass(1, RIGHT, 2)
    gradients(1, RIGHT, 2, False, False)
    far(1, 1)
    backward_pass(1, OPPOSITE, 1)
    gradients(1, OPPOSITE, 1, False, True)
    for copy in stores[2:]:
        copy.start()

    for t in range(2):
        for k in range(2):
            left_out = CAP if k == 0 else 0
            settle(send.at[t, pl.ds(left_out, shard - left_out)], a_send.at[t, k])
            for i in range(6):
                settle(held.at[t, k, rows_of(OWN, 0)], y_send.at[t, k, i])
        for i in range(6):
            settle(via.at[t, 0], r_send.at[t, i])
        settle(ret_send.at[t, rest], e_send.at[t])
    for copy in stores:
        copy.wait()


def solution(mesh):
    n_section = mesh.shape["section"]
    window = mesh.shape["expert"] // SPLIT

    def per_device(tokens, routes, route_weights, cotangent, w_gate, w_up, w_down):
        _, n_tok, width = tokens.shape
        hidden = w_gate.shape[2]
        shard = window * CAP
        rows = SPLIT * shard
        step = 512 if width % 512 == 0 else 128
        vmem = pl.BlockSpec(memory_space=pltpu.VMEM)
        hbm = pl.BlockSpec(memory_space=pl.ANY)
        dma = pltpu.SemaphoreType.DMA
        flops = 2 * rows * width * hidden * 15
        outs = pl.pallas_call(
            functools.partial(kernel, n_section, window, step),
            out_shape=(
                jax.ShapeDtypeStruct((n_tok, width), BF16),
                jax.ShapeDtypeStruct((n_tok, width), BF16),
                jax.ShapeDtypeStruct((width, hidden), BF16),
                jax.ShapeDtypeStruct((width, hidden), BF16),
                jax.ShapeDtypeStruct((hidden, width), BF16),
            ),
            in_specs=[hbm, vmem, vmem, hbm, hbm, hbm, hbm],
            out_specs=(hbm,) * 5,
            scratch_shapes=[
                pltpu.VMEM((n_tok, width), BF16),
                pltpu.VMEM((n_tok, width), BF16),
                pltpu.VMEM((width, hidden), BF16),
                pltpu.VMEM((width, hidden), BF16),
                pltpu.VMEM((hidden, width), BF16),
                pltpu.VMEM((2, shard, width), BF16),
                pltpu.VMEM((2, 2, rows, width), BF16),
                pltpu.VMEM((n_tok, shard), BF16),
                pltpu.VMEM((n_tok, shard), BF16),
                pltpu.VMEM((n_tok, shard), BF16),
                pltpu.VMEM((rows, hidden), F32),
                pltpu.VMEM((rows, hidden), F32),
                pltpu.VMEM((3, 2, rows, hidden), BF16),
                pltpu.VMEM((2, rows, width), BF16),
                pltpu.VMEM((2, 2, shard // 2, width), BF16),
                pltpu.VMEM((2, 2 * shard, width), BF16),
                pltpu.VMEM((2, shard, width), BF16),
                pltpu.VMEM((2, shard, width), BF16),
                pltpu.VMEM((width, hidden), F32),
                pltpu.VMEM((width, hidden), F32),
                pltpu.VMEM((hidden, width), F32),
                dma((5,)),
                dma((5,)),
                dma((2, 2)),
                dma((2, 2, 2)),
                dma((2, 2, 6)),
                dma((2, 2, 6)),
                dma((2, 6)),
                dma((2, 6)),
                dma((2,)),
                dma((2,)),
            ],
            compiler_params=pltpu.CompilerParams(
                collective_id=0, has_side_effects=True, vmem_limit_bytes=48 * 2**20
            ),
            cost_estimate=pl.CostEstimate(flops=flops, bytes_accessed=2 * 8 * n_tok * width, transcendentals=0),
        )(tokens[0], routes[0].T, route_weights[0].T, cotangent[0], w_gate[0], w_up[0], w_down[0])
        return tuple(out[None] for out in outs)

    return jax.shard_map(
        per_device,
        mesh=mesh,
        in_specs=(
            P("section", "expert", None),
            P("section", "expert", None),
            P("section", "expert", None),
            P("section", "expert", None),
            P("section", None, "expert"),
            P("section", None, "expert"),
            P("section", "expert", None),
        ),
        out_specs=(
            P("section", "expert", None),
            P("section", "expert", None),
            P("section", None, "expert"),
            P("section", None, "expert"),
            P("section", "expert", None),
        ),
        check_vma=False,
    )
```

```python
import functools

import jax
import jax.numpy as jnp
from jax import lax
from jax.experimental import pallas as pl
from jax.experimental.pallas import tpu as pltpu
from jax.sharding import PartitionSpec as P

SPLIT = 4
CAP = 16
MESH = pl.DeviceIdType.MESH
F32 = jnp.float32
BF16 = jnp.bfloat16

OWN, RIGHT, LEFT, OPPOSITE = range(4)
ACROSS = ((0, 0), (0, 1))


def nt(left, right):
    return lax.dot_general(left, right, (((1,), (1,)), ((), ())), preferred_element_type=F32)


def tn(left, right):
    return lax.dot_general(left, right, (((0,), (0,)), ((), ())), preferred_element_type=F32)


def nn(left, right):
    return jnp.dot(left, right, preferred_element_type=F32)


def kernel(
    n_section, window, step,
    tokens_hbm, routes, route_weights, cotangent_hbm, gate_hbm, up_hbm, down_hbm,
    mixed_hbm, grad_in_hbm, grad_gate_hbm, grad_up_hbm, grad_down_hbm,
    tokens, cotangent, w_gate, w_up, w_down, send, held, weights_hi, weights_lo, chosen,
    gate_val, up_val, act, part, via, last, ret_send, ret,
    sum_gate, sum_up, sum_down,
    in_sem, out_sem, a_send, a_recv, y_send, y_recv, r_send, r_recv, e_send, e_recv,
):
    group = lax.axis_index("section")
    index = lax.axis_index("expert")
    expert = index // SPLIT
    quarter = index % SPLIT
    mirror = n_section - 1 - group
    shard = window * CAP
    half = shard // 2
    n_tok, width = tokens.shape

    right = (group, expert * SPLIT + (quarter + 1) % SPLIT)
    left = (group, expert * SPLIT + (quarter + SPLIT - 1) % SPLIT)

    def at_expert(g, j):
        return (g, (expert + j) % window * SPLIT + quarter)

    sources = (tokens_hbm, cotangent_hbm, gate_hbm, up_hbm, down_hbm)
    places = (tokens, cotangent, w_gate, w_up, w_down)
    loads = [pltpu.make_async_copy(src, dst, in_sem.at[i]) for i, (src, dst) in enumerate(zip(sources, places))]
    results = (mixed_hbm, grad_in_hbm, grad_gate_hbm, grad_up_hbm, grad_down_hbm)
    stores = [pltpu.make_async_copy(src, dst, out_sem.at[i]) for i, (src, dst) in enumerate(zip(places, results))]
    for copy in loads[:2]:
        copy.start()

    barrier = pltpu.get_barrier_semaphore()
    friends = [right, left]
    friends += [at_expert(group, j) for j in range(1, window)]
    friends += [at_expert(mirror, j) for j in range(window)]
    for friend in friends:
        pl.semaphore_signal(barrier, inc=1, device_id=friend, device_id_type=MESH)

    def remote(src, dst, send_sem, recv_sem, device):
        pltpu.make_async_remote_copy(
            src_ref=src, dst_ref=dst, send_sem=send_sem, recv_sem=recv_sem,
            device_id=device, device_id_type=MESH,
        ).start()

    def settle(ref, sem):
        pltpu.make_async_copy(ref, ref, sem).wait()

    def chunks(body, total=width):
        def run(i, carry):
            body(pl.ds(pl.multiple_of(i * step, step), step))
            return carry

        lax.fori_loop(0, total // step, run, 0)

    row = lax.broadcasted_iota(jnp.int32, (shard, n_tok), 0)
    wanted = (expert + row // CAP) % window
    hits = jnp.zeros((shard, n_tok), F32)
    weight = jnp.zeros((shard, n_tok), F32)
    for k in range(routes.shape[0]):
        same = routes[k : k + 1] == wanted
        hits = jnp.where(same, 1.0, hits)
        weight = weight + jnp.where(same, route_weights[k : k + 1], 0.0)
    before = lax.broadcasted_iota(jnp.int32, (n_tok, n_tok), 0) < lax.broadcasted_iota(
        jnp.int32, (n_tok, n_tok), 1
    )
    slot = nn(hits.astype(BF16), jnp.where(before, 1.0, 0.0).astype(BF16))
    kept = (hits > 0.0) & (slot == (row % CAP).astype(F32))
    select = jnp.where(kept, 1.0, 0.0)
    weight = jnp.where(kept, weight, 0.0)
    select_t = select.astype(BF16)
    scale = jnp.sum(weight, axis=1, keepdims=True)

    def pick_rows(at):
        send[0, :, at] = nn(select_t, tokens[:, at]).astype(BF16)
        held[0, 0, :CAP, at] = send[0, :CAP, at]

    def pick_scaled(at):
        send[1, :, at] = (scale * nn(select_t, cotangent[:, at])).astype(BF16)
        held[1, 0, :CAP, at] = send[1, :CAP, at]

    def block(j):
        return pl.ds(j * CAP, CAP)

    def dispatch(t, k):
        g = (group, mirror)[k]
        for j in range(1 - k, window):
            remote(
                send.at[t, block(j)], held.at[t, k, block(j)],
                a_send.at[t, k], a_recv.at[t, k, j // (window // 2)], at_expert(g, j),
            )

    def rows_of(which, h=None):
        if h is None:
            return pl.ds(which * shard, shard)
        return pl.ds(which * shard + h * half, half)

    def both_ways(t, k, h, low, count):
        def part_of(which):
            return held.at[t, k, pl.ds(which * shard + h * half + low, count)]

        remote(part_of(OWN), part_of(LEFT), y_send.at[t, k, h], y_recv.at[t, k, h], right)
        remote(part_of(OWN), part_of(RIGHT), y_send.at[t, k, 2 + h], y_recv.at[t, k, 2 + h], left)

    def gather(t, k):
        for h in range(2):
            skip = CAP if k == 0 and h == 0 else 0
            settle(held.at[t, k, pl.ds(h * half + skip, half - skip)], a_recv.at[t, k, h])
            both_ways(t, k, h, skip, half - skip)

    def forward(t, k):
        from_left = [(held.at[t, k, rows_of(LEFT, h)], y_recv.at[t, k, h]) for h in range(2)]
        from_right = [(held.at[t, k, rows_of(RIGHT, h)], y_recv.at[t, k, 2 + h]) for h in range(2)]
        settle(*from_right[0])
        if k == 0 or (t, 0) not in ACROSS:
            remote(from_right[0][0], held.at[t, k, rows_of(OPPOSITE, 0)], y_send.at[t, k, 4], y_recv.at[t, k, 4], left)
        settle(*from_left[0])
        settle(*from_left[1])
        if k == 0 or (t, 1) not in ACROSS:
            remote(from_left[1][0], held.at[t, k, rows_of(OPPOSITE, 1)], y_send.at[t, k, 5], y_recv.at[t, k, 5], right)
        settle(*from_right[1])

    def far(t, k):
        for h in range(2):
            shard_half = held.at[t, k, rows_of(OPPOSITE, h)]
            settle(shard_half, y_recv.at[t, k, 4 + h])
            if k == 0 and (t, h) in ACROSS:
                remote(
                    shard_half, held.at[t, 1, rows_of(OPPOSITE, h)],
                    y_send.at[t, 1, 4 + h], y_recv.at[t, 1, 4 + h], at_expert(mirror, 0),
                )

    def forward_pass(k, first, count):
        rows = pl.ds(first * shard, count * shard)
        x = held[0, k, rows]
        gate_val[rows] = nn(x, w_gate[...])
        up_val[rows] = nn(x, w_up[...])

    def backward_pass(k, first, count):
        rows = pl.ds(first * shard, count * shard)
        dh = nt(held[1, k, rows], w_down[...])
        gate, up = gate_val[rows], up_val[rows]
        sig = jax.nn.sigmoid(gate)
        act[0, k, rows] = (gate * sig * up).astype(BF16)
        act[1, k, rows] = (dh * up * sig * (1.0 + gate * (1.0 - sig))).astype(BF16)
        act[2, k, rows] = (dh * gate * sig).astype(BF16)

    def parts(first, count):
        rows = pl.ds(first * shard, count * shard)

        def one(at):
            part[0, rows, at] = nn(act[0, 0, rows], w_down[:, at]).astype(BF16)
            part[1, rows, at] = (
                nt(act[1, 0, rows], w_gate[at, :]) + nt(act[2, 0, rows], w_up[at, :])
            ).astype(BF16)

        chunks(one)

    def gradients(k, first, count, start, stop):
        rows = pl.ds(first * shard, count * shard)

        def one(at):
            x, g = held[0, k, rows, at], held[1, k, rows, at]
            terms = (tn(x, act[1, k, rows]), tn(x, act[2, k, rows]), tn(act[0, k, rows], g))
            where = ((at, slice(None)), (at, slice(None)), (slice(None), at))
            for total, out, term, place in zip((sum_gate, sum_up, sum_down), places[2:], terms, where):
                if not start:
                    term = total[place] + term
                if stop:
                    out[place] = term.astype(BF16)
                else:
                    total[place] = term

        chunks(one)

    loads[0].wait()
    chunks(pick_rows)
    pl.semaphore_wait(barrier, len(friends))
    dispatch(0, 0)
    both_ways(0, 0, 0, 0, CAP)
    loads[1].wait()
    chunks(pick_scaled)
    dispatch(1, 0)
    both_ways(1, 0, 0, 0, CAP)
    for copy in loads[2:]:
        copy.start()
    weight_t = jnp.transpose(weight)
    high = weight_t.astype(BF16)
    weights_hi[...] = high
    weights_lo[...] = (weight_t - high.astype(F32)).astype(BF16)
    chosen[...] = jnp.transpose(select).astype(BF16)

    gather(0, 0)
    dispatch(0, 1)
    gather(1, 0)
    dispatch(1, 1)
    for copy in loads[2:]:
        copy.wait()
    forward_pass(0, OWN, 1)
    forward(0, 0)
    backward_pass(0, OWN, 1)
    parts(OWN, 1)
    forward_pass(0, RIGHT, 2)
    forward(1, 0)
    far(0, 0)
    backward_pass(0, RIGHT, 2)
    parts(RIGHT, 2)

    for t in range(2):
        remote(part.at[t, rows_of(RIGHT, 1)], last.at[t, rows_of(0, 1)], r_send.at[t, 3], r_recv.at[t, 3], right)
        remote(part.at[t, rows_of(LEFT, 0)], last.at[t, rows_of(1, 0)], r_send.at[t, 4], r_recv.at[t, 4], left)
    forward_pass(0, OPPOSITE, 1)
    far(1, 0)
    backward_pass(0, OPPOSITE, 1)
    parts(OPPOSITE, 1)
    for t in range(2):
        remote(part.at[t, rows_of(OPPOSITE, 0)], via.at[t, 0], r_send.at[t, 0], r_recv.at[t, 0], right)
        remote(part.at[t, rows_of(OPPOSITE, 1)], via.at[t, 1], r_send.at[t, 1], r_recv.at[t, 1], left)
    gather(0, 1)
    forward_pass(1, OWN, 1)

    for t in range(2):
        settle(via.at[t, 0], r_recv.at[t, 0])
        rows = rows_of(RIGHT, 0)
        part[t, rows] = (part[t, rows].astype(F32) + via[t, 0].astype(F32)).astype(BF16)
        remote(part.at[t, rows], last.at[t, rows_of(0, 0)], r_send.at[t, 2], r_recv.at[t, 2], right)
        settle(via.at[t, 1], r_recv.at[t, 1])
        rows = rows_of(LEFT, 1)
        part[t, rows] = (part[t, rows].astype(F32) + via[t, 1].astype(F32)).astype(BF16)
        remote(part.at[t, rows], last.at[t, rows_of(1, 1)], r_send.at[t, 5], r_recv.at[t, 5], left)

    gather(1, 1)
    gradients(0, OWN, 4, True, False)

    for t in range(2):
        for h in range(2):
            settle(last.at[t, rows_of(0, h)], r_recv.at[t, 2 + h])
            settle(last.at[t, rows_of(1, h)], r_recv.at[t, 4 + h])
            rows = rows_of(OWN, h)
            total = part[t, rows].astype(F32) + last[t, rows_of(0, h)].astype(F32) + last[t, rows_of(1, h)].astype(F32)
            ret_send[t, rows] = total.astype(BF16)
        ret[t, :CAP] = ret_send[t, :CAP]
        for j in range(1, window):
            remote(
                ret_send.at[t, block(j)], ret.at[t, block(j)],
                e_send.at[t], e_recv.at[t], at_expert(group, window - j),
            )

    backward_pass(1, OWN, 1)
    gradients(1, OWN, 1, False, False)
    forward(0, 1)
    forward_pass(1, RIGHT, 2)
    far(0, 1)
    forward_pass(1, OPPOSITE, 1)

    rest = pl.ds(CAP, shard - CAP)
    settle(ret.at[0, rest], e_recv.at[0])

    def combine_out(at):
        tokens[:, at] = (nn(weights_hi[...], ret[0, :, at]) + nn(weights_lo[...], ret[0, :, at])).astype(BF16)

    chunks(combine_out)
    stores[0].start()
    settle(ret.at[1, rest], e_recv.at[1])

    def combine_back(at):
        cotangent[:, at] = nn(chosen[...], ret[1, :, at]).astype(BF16)

    chunks(combine_back)
    stores[1].start()

    forward(1, 1)
    backward_pass(1, RIGHT, 2)
    gradients(1, RIGHT, 2, False, False)
    far(1, 1)
    backward_pass(1, OPPOSITE, 1)
    gradients(1, OPPOSITE, 1, False, True)
    for copy in stores[2:]:
        copy.start()

    for t in range(2):
        for k in range(2):
            left_out = CAP if k == 0 else 0
            settle(send.at[t, pl.ds(left_out, shard - left_out)], a_send.at[t, k])
            for i in range(6):
                settle(held.at[t, k, rows_of(OWN, 0)], y_send.at[t, k, i])
        for i in range(6):
            settle(via.at[t, 0], r_send.at[t, i])
        settle(ret_send.at[t, rest], e_send.at[t])
    for copy in stores:
        copy.wait()


def hand_over(*refs):
    n = len(refs) // 2
    copies = [pltpu.make_async_copy(refs[i], refs[n + i], refs[-1].at[i]) for i in range(n)]
    for copy in copies:
        copy.start()
    for copy in copies:
        copy.wait()


def solution(mesh):
    n_section = mesh.shape["section"]
    window = mesh.shape["expert"] // SPLIT

    def per_device(tokens, routes, route_weights, cotangent, w_gate, w_up, w_down):
        _, n_tok, width = tokens.shape
        hidden = w_gate.shape[2]
        shard = window * CAP
        rows = SPLIT * shard
        step = 512 if width % 512 == 0 else 128
        vmem = pl.BlockSpec(memory_space=pltpu.VMEM)
        hbm = pl.BlockSpec(memory_space=pl.ANY)
        dma = pltpu.SemaphoreType.DMA
        flops = 2 * rows * width * hidden * 15
        outs = pl.pallas_call(
            functools.partial(kernel, n_section, window, step),
            out_shape=(
                jax.ShapeDtypeStruct((n_tok, width), BF16),
                jax.ShapeDtypeStruct((n_tok, width), BF16),
                jax.ShapeDtypeStruct((width, hidden), BF16),
                jax.ShapeDtypeStruct((width, hidden), BF16),
                jax.ShapeDtypeStruct((hidden, width), BF16),
            ),
            in_specs=[hbm, vmem, vmem, hbm, hbm, hbm, hbm],
            out_specs=(hbm,) * 5,
            scratch_shapes=[
                pltpu.VMEM((n_tok, width), BF16),
                pltpu.VMEM((n_tok, width), BF16),
                pltpu.VMEM((width, hidden), BF16),
                pltpu.VMEM((width, hidden), BF16),
                pltpu.VMEM((hidden, width), BF16),
                pltpu.VMEM((2, shard, width), BF16),
                pltpu.VMEM((2, 2, rows, width), BF16),
                pltpu.VMEM((n_tok, shard), BF16),
                pltpu.VMEM((n_tok, shard), BF16),
                pltpu.VMEM((n_tok, shard), BF16),
                pltpu.VMEM((rows, hidden), F32),
                pltpu.VMEM((rows, hidden), F32),
                pltpu.VMEM((3, 2, rows, hidden), BF16),
                pltpu.VMEM((2, rows, width), BF16),
                pltpu.VMEM((2, 2, shard // 2, width), BF16),
                pltpu.VMEM((2, 2 * shard, width), BF16),
                pltpu.VMEM((2, shard, width), BF16),
                pltpu.VMEM((2, shard, width), BF16),
                pltpu.VMEM((width, hidden), F32),
                pltpu.VMEM((width, hidden), F32),
                pltpu.VMEM((hidden, width), F32),
                dma((5,)),
                dma((5,)),
                dma((2, 2)),
                dma((2, 2, 2)),
                dma((2, 2, 6)),
                dma((2, 2, 6)),
                dma((2, 6)),
                dma((2, 6)),
                dma((2,)),
                dma((2,)),
            ],
            compiler_params=pltpu.CompilerParams(
                collective_id=0, has_side_effects=True, vmem_limit_bytes=93 * 2**19
            ),
            cost_estimate=pl.CostEstimate(flops=flops, bytes_accessed=2 * 8 * n_tok * width, transcendentals=0),
        )(tokens[0], routes[0].T, route_weights[0].T, cotangent[0], w_gate[0], w_up[0], w_down[0])
        outs = pl.pallas_call(
            hand_over,
            out_shape=tuple(jax.ShapeDtypeStruct(out.shape, out.dtype) for out in outs),
            in_specs=[hbm] * 5,
            out_specs=(hbm,) * 5,
            scratch_shapes=[dma((5,))],
            compiler_params=pltpu.CompilerParams(vmem_limit_bytes=2**20),
        )(*outs)
        return tuple(out[None] for out in outs)

    return jax.shard_map(
        per_device,
        mesh=mesh,
        in_specs=(
            P("section", "expert", None),
            P("section", "expert", None),
            P("section", "expert", None),
            P("section", "expert", None),
            P("section", None, "expert"),
            P("section", None, "expert"),
            P("section", "expert", None),
        ),
        out_specs=(
            P("section", "expert", None),
            P("section", "expert", None),
            P("section", None, "expert"),
            P("section", None, "expert"),
            P("section", "expert", None),
        ),
        check_vma=False,
    )
```

```python
import functools

import jax
import jax.numpy as jnp
from jax import lax
from jax.experimental import pallas as pl
from jax.experimental.pallas import tpu as pltpu
from jax.sharding import PartitionSpec as P

SPLIT = 4
CAP = 16
MESH = pl.DeviceIdType.MESH
F32 = jnp.float32
BF16 = jnp.bfloat16

OWN, RIGHT, LEFT, OPPOSITE = range(4)
ACROSS = (4, 1)


def nt(left, right):
    return lax.dot_general(left, right, (((1,), (1,)), ((), ())), preferred_element_type=F32)


def tn(left, right):
    return lax.dot_general(left, right, (((0,), (0,)), ((), ())), preferred_element_type=F32)


def nn(left, right):
    return jnp.dot(left, right, preferred_element_type=F32)


def kernel(
    n_section, window, step,
    tokens_hbm, routes, route_weights, cotangent_hbm, gate_hbm, up_hbm, down_hbm,
    mixed_hbm, grad_in_hbm, grad_gate_hbm, grad_up_hbm, grad_down_hbm,
    tokens, cotangent, w_gate, w_up, w_down, send, held, weights_hi, weights_lo, chosen,
    gate_val, up_val, act, part, via, last, ret_send, ret,
    sum_gate, sum_up, sum_down,
    in_sem, out_sem, a_send, a_recv, y_send, y_recv, r_send, r_recv, e_send, e_recv,
):
    group = lax.axis_index("section")
    index = lax.axis_index("expert")
    expert = index // SPLIT
    quarter = index % SPLIT
    mirror = n_section - 1 - group
    shard = window * CAP
    half = shard // 2
    n_tok, width = tokens.shape

    right = (group, expert * SPLIT + (quarter + 1) % SPLIT)
    left = (group, expert * SPLIT + (quarter + SPLIT - 1) % SPLIT)

    def at_expert(g, j):
        return (g, (expert + j) % window * SPLIT + quarter)

    sources = (tokens_hbm, cotangent_hbm, gate_hbm, up_hbm, down_hbm)
    places = (tokens, cotangent, w_gate, w_up, w_down)
    loads = [pltpu.make_async_copy(src, dst, in_sem.at[i]) for i, (src, dst) in enumerate(zip(sources, places))]
    results = (mixed_hbm, grad_in_hbm, grad_gate_hbm, grad_up_hbm, grad_down_hbm)
    stores = [pltpu.make_async_copy(src, dst, out_sem.at[i]) for i, (src, dst) in enumerate(zip(places, results))]
    for copy in loads[:2]:
        copy.start()

    barrier = pltpu.get_barrier_semaphore()
    friends = [right, left]
    friends += [at_expert(group, j) for j in range(1, window)]
    friends += [at_expert(mirror, j) for j in range(window)]
    for friend in friends:
        pl.semaphore_signal(barrier, inc=1, device_id=friend, device_id_type=MESH)

    def remote(src, dst, send_sem, recv_sem, device):
        pltpu.make_async_remote_copy(
            src_ref=src, dst_ref=dst, send_sem=send_sem, recv_sem=recv_sem,
            device_id=device, device_id_type=MESH,
        ).start()

    def settle(ref, sem):
        pltpu.make_async_copy(ref, ref, sem).wait()

    def chunks(body, total=width):
        def run(i, carry):
            body(pl.ds(pl.multiple_of(i * step, step), step))
            return carry

        lax.fori_loop(0, total // step, run, 0)

    row = lax.broadcasted_iota(jnp.int32, (shard, n_tok), 0)
    wanted = (expert + row // CAP) % window
    hits = jnp.zeros((shard, n_tok), F32)
    weight = jnp.zeros((shard, n_tok), F32)
    for k in range(routes.shape[0]):
        same = routes[k : k + 1] == wanted
        hits = jnp.where(same, 1.0, hits)
        weight = weight + jnp.where(same, route_weights[k : k + 1], 0.0)
    before = lax.broadcasted_iota(jnp.int32, (n_tok, n_tok), 0) < lax.broadcasted_iota(
        jnp.int32, (n_tok, n_tok), 1
    )
    slot = nn(hits.astype(BF16), jnp.where(before, 1.0, 0.0).astype(BF16))
    kept = (hits > 0.0) & (slot == (row % CAP).astype(F32))
    select = jnp.where(kept, 1.0, 0.0)
    weight = jnp.where(kept, weight, 0.0)
    select_t = select.astype(BF16)
    scale = jnp.sum(weight, axis=1, keepdims=True)

    def pick_rows(at):
        send[0, :, at] = nn(select_t, tokens[:, at]).astype(BF16)
        held[0, 0, :CAP, at] = send[0, :CAP, at]

    def pick_scaled(at):
        send[1, :, at] = (scale * nn(select_t, cotangent[:, at])).astype(BF16)
        held[1, 0, :CAP, at] = send[1, :CAP, at]

    def block(j):
        return pl.ds(j * CAP, CAP)

    def dispatch(t, k):
        g = (group, mirror)[k]
        for j in range(1 - k, window):
            remote(
                send.at[t, block(j)], held.at[t, k, block(j)],
                a_send.at[t, k], a_recv.at[t, k, j // (window // 2)], at_expert(g, j),
            )

    def rows_of(which, h=None):
        if h is None:
            return pl.ds(which * shard, shard)
        return pl.ds(which * shard + h * half, half)

    def both_ways(t, k, h, low, count):
        def part_of(which):
            return held.at[t, k, pl.ds(which * shard + h * half + low, count)]

        remote(part_of(OWN), part_of(LEFT), y_send.at[t, k, h], y_recv.at[t, k, h], right)
        remote(part_of(OWN), part_of(RIGHT), y_send.at[t, k, 2 + h], y_recv.at[t, k, 2 + h], left)

    def gather(t, k):
        for h in range(2):
            skip = CAP if k == 0 and h == 0 else 0
            settle(held.at[t, k, pl.ds(h * half + skip, half - skip)], a_recv.at[t, k, h])
            both_ways(t, k, h, skip, half - skip)

    def hand_on(t, k, h, which, device):
        count = half - k * ACROSS[t] * CAP
        if count > 0:
            rows = [held.at[t, k, pl.ds(w * shard + h * half, count)] for w in (which, OPPOSITE)]
            remote(*rows, y_send.at[t, k, 4 + h], y_recv.at[t, k, 4 + h], device)

    def forward(t, k):
        from_left = [(held.at[t, k, rows_of(LEFT, h)], y_recv.at[t, k, h]) for h in range(2)]
        from_right = [(held.at[t, k, rows_of(RIGHT, h)], y_recv.at[t, k, 2 + h]) for h in range(2)]
        settle(*from_right[0])
        hand_on(t, k, 0, RIGHT, left)
        settle(*from_left[0])
        settle(*from_left[1])
        hand_on(t, k, 1, LEFT, right)
        settle(*from_right[1])

    def far(t, k):
        for h in range(2):
            shard_half = held.at[t, k, rows_of(OPPOSITE, h)]
            settle(shard_half, y_recv.at[t, k, 4 + h])
            if k == 0 and ACROSS[t] > 0:
                count = ACROSS[t] * CAP
                rows = pl.ds(OPPOSITE * shard + (h + 1) * half - count, count)
                remote(
                    held.at[t, 0, rows], held.at[t, 1, rows],
                    y_send.at[t, 1, 4 + h], y_recv.at[t, 1, 4 + h], at_expert(mirror, 0),
                )

    def forward_pass(k, first, count):
        rows = pl.ds(first * shard, count * shard)
        x = held[0, k, rows]
        gate_val[rows] = nn(x, w_gate[...])
        up_val[rows] = nn(x, w_up[...])

    def backward_pass(k, first, count):
        rows = pl.ds(first * shard, count * shard)
        dh = nt(held[1, k, rows], w_down[...])
        gate, up = gate_val[rows], up_val[rows]
        sig = jax.nn.sigmoid(gate)
        act[0, k, rows] = (gate * sig * up).astype(BF16)
        act[1, k, rows] = (dh * up * sig * (1.0 + gate * (1.0 - sig))).astype(BF16)
        act[2, k, rows] = (dh * gate * sig).astype(BF16)

    def parts(first, count):
        rows = pl.ds(first * shard, count * shard)

        def one(at):
            part[0, rows, at] = nn(act[0, 0, rows], w_down[:, at]).astype(BF16)
            part[1, rows, at] = (
                nt(act[1, 0, rows], w_gate[at, :]) + nt(act[2, 0, rows], w_up[at, :])
            ).astype(BF16)

        chunks(one)

    def gradients(k, first, count, start, stop):
        rows = pl.ds(first * shard, count * shard)

        def one(at):
            x, g = held[0, k, rows, at], held[1, k, rows, at]
            terms = (tn(x, act[1, k, rows]), tn(x, act[2, k, rows]), tn(act[0, k, rows], g))
            where = ((at, slice(None)), (at, slice(None)), (slice(None), at))
            for total, out, term, place in zip((sum_gate, sum_up, sum_down), places[2:], terms, where):
                if not start:
                    term = total[place] + term
                if stop:
                    out[place] = term.astype(BF16)
                else:
                    total[place] = term

        chunks(one)

    loads[0].wait()
    chunks(pick_rows)
    pl.semaphore_wait(barrier, len(friends))
    dispatch(0, 0)
    both_ways(0, 0, 0, 0, CAP)
    loads[1].wait()
    chunks(pick_scaled)
    dispatch(1, 0)
    both_ways(1, 0, 0, 0, CAP)
    for copy in loads[2:]:
        copy.start()
    weight_t = jnp.transpose(weight)
    high = weight_t.astype(BF16)
    weights_hi[...] = high
    weights_lo[...] = (weight_t - high.astype(F32)).astype(BF16)
    chosen[...] = jnp.transpose(select).astype(BF16)

    gather(0, 0)
    dispatch(0, 1)
    gather(1, 0)
    dispatch(1, 1)
    for copy in loads[2:]:
        copy.wait()
    forward_pass(0, OWN, 1)
    forward(0, 0)
    backward_pass(0, OWN, 1)
    parts(OWN, 1)
    forward_pass(0, RIGHT, 2)
    forward(1, 0)
    far(0, 0)
    backward_pass(0, RIGHT, 2)
    parts(RIGHT, 2)

    for t in range(2):
        remote(part.at[t, rows_of(RIGHT, 1)], last.at[t, rows_of(0, 1)], r_send.at[t, 3], r_recv.at[t, 3], right)
        remote(part.at[t, rows_of(LEFT, 0)], last.at[t, rows_of(1, 0)], r_send.at[t, 4], r_recv.at[t, 4], left)
    forward_pass(0, OPPOSITE, 1)
    far(1, 0)
    backward_pass(0, OPPOSITE, 1)
    parts(OPPOSITE, 1)
    for t in range(2):
        remote(part.at[t, rows_of(OPPOSITE, 0)], via.at[t, 0], r_send.at[t, 0], r_recv.at[t, 0], right)
        remote(part.at[t, rows_of(OPPOSITE, 1)], via.at[t, 1], r_send.at[t, 1], r_recv.at[t, 1], left)
    gather(0, 1)
    forward_pass(1, OWN, 1)

    for t in range(2):
        settle(via.at[t, 0], r_recv.at[t, 0])
        rows = rows_of(RIGHT, 0)
        part[t, rows] = (part[t, rows].astype(F32) + via[t, 0].astype(F32)).astype(BF16)
        remote(part.at[t, rows], last.at[t, rows_of(0, 0)], r_send.at[t, 2], r_recv.at[t, 2], right)
        settle(via.at[t, 1], r_recv.at[t, 1])
        rows = rows_of(LEFT, 1)
        part[t, rows] = (part[t, rows].astype(F32) + via[t, 1].astype(F32)).astype(BF16)
        remote(part.at[t, rows], last.at[t, rows_of(1, 1)], r_send.at[t, 5], r_recv.at[t, 5], left)

    gather(1, 1)
    gradients(0, OWN, 4, True, False)

    for t in range(2):
        for h in range(2):
            settle(last.at[t, rows_of(0, h)], r_recv.at[t, 2 + h])
            settle(last.at[t, rows_of(1, h)], r_recv.at[t, 4 + h])
            rows = rows_of(OWN, h)
            total = part[t, rows].astype(F32) + last[t, rows_of(0, h)].astype(F32) + last[t, rows_of(1, h)].astype(F32)
            ret_send[t, rows] = total.astype(BF16)
        ret[t, :CAP] = ret_send[t, :CAP]
        for j in range(1, window):
            remote(
                ret_send.at[t, block(j)], ret.at[t, block(j)],
                e_send.at[t], e_recv.at[t], at_expert(group, window - j),
            )

    backward_pass(1, OWN, 1)
    gradients(1, OWN, 1, False, False)
    forward(0, 1)
    forward_pass(1, RIGHT, 2)
    far(0, 1)
    forward_pass(1, OPPOSITE, 1)

    rest = pl.ds(CAP, shard - CAP)
    settle(ret.at[0, rest], e_recv.at[0])

    def combine_out(at):
        tokens[:, at] = (nn(weights_hi[...], ret[0, :, at]) + nn(weights_lo[...], ret[0, :, at])).astype(BF16)

    chunks(combine_out)
    stores[0].start()
    settle(ret.at[1, rest], e_recv.at[1])

    def combine_back(at):
        cotangent[:, at] = nn(chosen[...], ret[1, :, at]).astype(BF16)

    chunks(combine_back)
    stores[1].start()

    forward(1, 1)
    backward_pass(1, RIGHT, 2)
    gradients(1, RIGHT, 2, False, False)
    far(1, 1)
    backward_pass(1, OPPOSITE, 1)
    gradients(1, OPPOSITE, 1, False, True)
    for copy in stores[2:]:
        copy.start()

    for t in range(2):
        for k in range(2):
            left_out = CAP if k == 0 else 0
            settle(send.at[t, pl.ds(left_out, shard - left_out)], a_send.at[t, k])
            for i in range(6):
                settle(held.at[t, k, rows_of(OWN, 0)], y_send.at[t, k, i])
        for i in range(6):
            settle(via.at[t, 0], r_send.at[t, i])
        settle(ret_send.at[t, rest], e_send.at[t])
    for copy in stores:
        copy.wait()


def hand_over(*refs):
    n = len(refs) // 2
    copies = [pltpu.make_async_copy(refs[i], refs[n + i], refs[-1].at[i]) for i in range(n)]
    for copy in copies:
        copy.start()
    for copy in copies:
        copy.wait()


def solution(mesh):
    n_section = mesh.shape["section"]
    window = mesh.shape["expert"] // SPLIT

    def per_device(tokens, routes, route_weights, cotangent, w_gate, w_up, w_down):
        _, n_tok, width = tokens.shape
        hidden = w_gate.shape[2]
        shard = window * CAP
        rows = SPLIT * shard
        step = 512 if width % 512 == 0 else 128
        vmem = pl.BlockSpec(memory_space=pltpu.VMEM)
        hbm = pl.BlockSpec(memory_space=pl.ANY)
        dma = pltpu.SemaphoreType.DMA
        flops = 2 * rows * width * hidden * 15
        outs = pl.pallas_call(
            functools.partial(kernel, n_section, window, step),
            out_shape=(
                jax.ShapeDtypeStruct((n_tok, width), BF16),
                jax.ShapeDtypeStruct((n_tok, width), BF16),
                jax.ShapeDtypeStruct((width, hidden), BF16),
                jax.ShapeDtypeStruct((width, hidden), BF16),
                jax.ShapeDtypeStruct((hidden, width), BF16),
            ),
            in_specs=[hbm, vmem, vmem, hbm, hbm, hbm, hbm],
            out_specs=(hbm,) * 5,
            scratch_shapes=[
                pltpu.VMEM((n_tok, width), BF16),
                pltpu.VMEM((n_tok, width), BF16),
                pltpu.VMEM((width, hidden), BF16),
                pltpu.VMEM((width, hidden), BF16),
                pltpu.VMEM((hidden, width), BF16),
                pltpu.VMEM((2, shard, width), BF16),
                pltpu.VMEM((2, 2, rows, width), BF16),
                pltpu.VMEM((n_tok, shard), BF16),
                pltpu.VMEM((n_tok, shard), BF16),
                pltpu.VMEM((n_tok, shard), BF16),
                pltpu.VMEM((rows, hidden), F32),
                pltpu.VMEM((rows, hidden), F32),
                pltpu.VMEM((3, 2, rows, hidden), BF16),
                pltpu.VMEM((2, rows, width), BF16),
                pltpu.VMEM((2, 2, shard // 2, width), BF16),
                pltpu.VMEM((2, 2 * shard, width), BF16),
                pltpu.VMEM((2, shard, width), BF16),
                pltpu.VMEM((2, shard, width), BF16),
                pltpu.VMEM((width, hidden), F32),
                pltpu.VMEM((width, hidden), F32),
                pltpu.VMEM((hidden, width), F32),
                dma((5,)),
                dma((5,)),
                dma((2, 2)),
                dma((2, 2, 2)),
                dma((2, 2, 6)),
                dma((2, 2, 6)),
                dma((2, 6)),
                dma((2, 6)),
                dma((2,)),
                dma((2,)),
            ],
            compiler_params=pltpu.CompilerParams(
                collective_id=0, has_side_effects=True, vmem_limit_bytes=93 * 2**19
            ),
            cost_estimate=pl.CostEstimate(flops=flops, bytes_accessed=2 * 8 * n_tok * width, transcendentals=0),
        )(tokens[0], routes[0].T, route_weights[0].T, cotangent[0], w_gate[0], w_up[0], w_down[0])
        outs = pl.pallas_call(
            hand_over,
            out_shape=tuple(jax.ShapeDtypeStruct(out.shape, out.dtype) for out in outs),
            in_specs=[hbm] * 5,
            out_specs=(hbm,) * 5,
            scratch_shapes=[dma((5,))],
            compiler_params=pltpu.CompilerParams(vmem_limit_bytes=2**20),
        )(*outs)
        return tuple(out[None] for out in outs)

    return jax.shard_map(
        per_device,
        mesh=mesh,
        in_specs=(
            P("section", "expert", None),
            P("section", "expert", None),
            P("section", "expert", None),
            P("section", "expert", None),
            P("section", None, "expert"),
            P("section", None, "expert"),
            P("section", "expert", None),
        ),
        out_specs=(
            P("section", "expert", None),
            P("section", "expert", None),
            P("section", None, "expert"),
            P("section", None, "expert"),
            P("section", "expert", None),
        ),
        check_vma=False,
    )
```
